256 devices in a mesh: gx: 16 (over z_hi, x), gy: 16 (over y, z_lo, core).
Axes of the slice: x: 4, y: 4, z: 8 (z_hi: 4, z_lo: 2; z = z_hi * 2 + z_lo), core: 2. Of those that a mesh axis runs over, the one named last changes fastest.
Arguments:
- field: bfloat16 [768, 128, 1536], P(None, 'gy', 'gx'), may hold values from -8 to 8
- norm_field: float32 [768, 128, 1536], P(('gx', 'gy')), may hold values from 0.5 to 2
- vertical: float32 [2, 64, 64], replicated, may hold values from -0.75 to 0.75
- x_filter: bfloat16 [1536, 1536], replicated, may hold values from -2 to 2
- y_filter: bfloat16 [768, 768], replicated, may hold values from -2 to 2
Outputs:
- covaried: bfloat16 [768, 128, 1536], P(None, 'gy', 'gx')
The draws below stay inside these ranges and needn't reach their ends.
All inputs are finite; a program needn't handle non-finite values.
Results may differ from the reference program's by a relative error of at most 0.0075.
Values may be sent and summed in bfloat16 or wider, within the bound.
No kernel may reach another device: no remote copies, remote signals or barrier semaphores. Data moves between devices by JAX's collectives and lax.ppermute only.
A program may use at most 64 MiB of HBM per device.

```python
import math
import jax
import jax.numpy as jnp
from jax import lax

NX = 1536
NY = 768
LEVELS = 64
SPECIES = 2
COMPONENTS = 128


def draw_field(key, part):
    key = jax.random.fold_in(key, 11)
    first_key = jax.random.fold_in(key, 0)
    base = jax.random.normal(first_key, (NY, SPECIES * LEVELS, NX), jnp.float32)
    values = jnp.clip(base, -6.0, 6.0)
    return values.astype(jnp.bfloat16)


def draw_x_filter(key, part):
    key = jax.random.fold_in(key, 23)
    spots = jnp.arange(NX, dtype=jnp.float32)
    reach = NX / 4.0
    envelope = jnp.exp(-jnp.abs(spots[:, None] - spots[None, :]) / reach)
    rough = jnp.clip(jax.random.normal(key, (NX, NX), jnp.float32), -3.0, 3.0)
    return (envelope * rough / math.sqrt(reach)).astype(jnp.bfloat16)


def draw_y_filter(key, part):
    key = jax.random.fold_in(key, 29)
    spots = jnp.arange(NY, dtype=jnp.float32)
    reach = NY / 4.0
    envelope = jnp.exp(-jnp.abs(spots[:, None] - spots[None, :]) / reach)
    rough = jnp.clip(jax.random.normal(key, (NY, NY), jnp.float32), -3.0, 3.0)
    return (envelope * rough / math.sqrt(reach)).astype(jnp.bfloat16)


def shard_levels(key, extent, shards, smallest, high):
    level = 1.0
    for dim, shards_of in shards:
        steps = jax.random.uniform(jax.random.fold_in(jax.random.fold_in(key, 6), dim), (shards_of,), jnp.float32, smallest / len(shards), high / len(shards))
        level = level * jnp.repeat(jnp.exp(steps), extent[dim] // shards_of).reshape((-1,) + (1,) * (len(extent) - 1 - dim))
    return level


def scatter_about(key, shape, spread, most, kind=jnp.bfloat16):
    values = spread * jax.random.normal(key, shape, jnp.float32)
    return jnp.clip(values, min=-most, max=most).astype(kind)


def setup_inputs(seed: int = 0) -> dict:
    splits = jax.random.split(jax.random.key(seed), 6)
    return {
        "field": draw_field(jax.random.fold_in(splits[5], 71), 0),
        "norm_field": jnp.clip(jnp.exp(math.log(2.0) - 1.3862944 * jax.random.uniform(splits[1], (NY, COMPONENTS, NX), jnp.float32) ** shard_levels(splits[1], (NY, COMPONENTS, NX), ((0, 256),), -0.2, 0.2)), 0.5, 2.0),
        "vertical": scatter_about(splits[2], (SPECIES, LEVELS, LEVELS), LEVELS ** -0.5, 0.75, jnp.float32),
        "x_filter": draw_x_filter(jax.random.fold_in(splits[5], 71), 0),
        "y_filter": draw_y_filter(jax.random.fold_in(splits[5], 71), 0),
    }


def reference(field, norm_field, vertical, x_filter, y_filter):
    def one_species(index):
        start = (index * LEVELS).astype(jnp.int32)
        block = lax.dynamic_slice_in_dim(field, start, LEVELS, 1)
        scales = lax.dynamic_slice_in_dim(norm_field, start, LEVELS, 1)
        factor = vertical[index]
        first = jnp.dot(y_filter.T, block.reshape(NY, -1), preferred_element_type=jnp.float32)
        first = first.astype(jnp.bfloat16).reshape(NY, LEVELS, NX)
        second = jnp.dot(first.reshape(-1, NX), x_filter, preferred_element_type=jnp.float32)
        second = second.astype(jnp.bfloat16).reshape(NY, LEVELS, NX)
        scaled = scales * second.astype(jnp.float32)
        lowered = jnp.einsum("lk,ylx->ykx", factor, scaled, precision=lax.Precision.HIGHEST)
        raised = jnp.einsum("kl,ylx->ykx", factor, lowered, precision=lax.Precision.HIGHEST)
        middle = (scales * raised).astype(jnp.bfloat16)
        third = jnp.dot(middle.reshape(-1, NX), x_filter.T, preferred_element_type=jnp.float32)
        third = third.astype(jnp.bfloat16).reshape(NY, -1)
        result = jnp.dot(y_filter, third, preferred_element_type=jnp.float32)
        return result.astype(jnp.bfloat16).reshape(NY, LEVELS, NX)

    stacked = lax.map(one_species, jnp.arange(SPECIES, dtype=jnp.int32))
    return jnp.transpose(stacked, (1, 0, 2, 3)).reshape(NY, SPECIES * LEVELS, NX)
```

```python
import functools

import jax
import jax.numpy as jnp
import numpy as np
from jax import lax
from jax.experimental import pallas as pl
from jax.experimental.pallas import tpu as pltpu
from jax.sharding import PartitionSpec as P

LANES = 128
WIDTH = 96
PIECE = 32
MAIN = 6
ROWS = 3
COMPS = 8
MESSAGE = ROWS * MAIN
F32 = jnp.float32
BF16 = jnp.bfloat16


def dot(a, b, contract):
    return lax.dot_general(a, b, ((contract[:1], contract[1:]), ((), ())), preferred_element_type=F32)


def spread_kernel(field_ref, filter_ref, out_ref, rows_ref):
    filt = filter_ref[...]
    lines = filt.shape[0]
    for pair in range(MAIN // 2):
        parts = []
        for j in (2 * pair, 2 * pair + 1):
            start = PIECE * (j % 3)
            parts += [field_ref[j], field_ref[MAIN + j // 3, start : start + PIECE, :]]
        first = dot(filt, jnp.concatenate(parts, axis=0), (0, 1))
        for half in range(2):
            rows_ref[pl.ds(2 * pair + half, lines, stride=MAIN), :] = first[:, half * LANES : (half + 1) * LANES]
    out_ref[...] = rows_ref[...].astype(BF16)


def gather_kernel(rows_in_ref, filter_ref, out_ref, rows_ref):
    filt = filter_ref[...]
    lines = filt.shape[0]
    rows_ref[...] = rows_in_ref[...].astype(F32)
    for j in range(MAIN):
        third = rows_ref[pl.ds(j, lines, stride=MAIN), :].astype(BF16)
        unit = (
            lax.broadcasted_iota(jnp.int32, (LANES, LANES), 0) == lax.broadcasted_iota(jnp.int32, (LANES, LANES), 1)
        ).astype(BF16)
        turned = dot(unit, third, (1, 1)).astype(BF16)
        result = dot(turned, filt, (1, 1)).astype(BF16)
        start = PIECE * (j % 3)
        out_ref[j] = result[:WIDTH]
        out_ref[MAIN + j // 3, start : start + PIECE, :] = result[WIDTH:]


def middle_kernel(rows_in_ref, filter_ref, norm_ref, vertical_ref, order_ref, out_ref, rows_ref, tail_ref, *, tiles, owners):
    filt = filter_ref[...]
    order = order_ref[...]
    block = owners * MESSAGE
    rest = block // 3
    rows_ref[...] = rows_in_ref[...].astype(F32)
    main = [rows_ref[block * g : block * (g + 1), :WIDTH] for g in range(tiles)]
    left = jnp.concatenate(main, axis=1).astype(BF16)
    tail = []
    for g in range(tiles):
        for t in range(3):
            tail.append(rows_ref[pl.ds(block * g + t, rest, stride=3), :][:, WIDTH:])
    below = jnp.concatenate(tail, axis=1).astype(BF16)
    lines = jnp.concatenate([left, below], axis=0)
    second = dot(lines, filt, (1, 0)).astype(BF16)
    second = dot(order, second, (1, 0))
    comps = norm_ref.shape[1]
    levels = vertical_ref.shape[1]
    raised = []
    for r in range(ROWS):
        for s in range(vertical_ref.shape[0]):
            factor = vertical_ref[s]
            weight = lax.dot_general(
                factor, factor, (((1,), (1,)), ((), ())), precision=lax.Precision.HIGHEST, preferred_element_type=F32
            )
            high = weight.astype(BF16)
            low = (weight - high.astype(F32)).astype(BF16)
            span = slice(s * levels, (s + 1) * levels)
            scales = norm_ref[r, span, :]
            scaled = scales * second[r * comps + s * levels : r * comps + (s + 1) * levels]
            upper = scaled.astype(BF16)
            under = (scaled - upper.astype(F32)).astype(BF16)
            product = dot(
                jnp.concatenate([high, high, low], axis=1), jnp.concatenate([upper, under, upper], axis=0), (1, 0)
            )
            raised.append((scales * product).astype(BF16))
    middle = jnp.concatenate(raised, axis=0)
    middle = dot(order, middle, (0, 0)).astype(BF16)
    third = dot(middle, filt, (1, 1))
    lane = lax.broadcasted_iota(jnp.int32, (block, LANES), 1)
    for g in range(tiles):
        start = WIDTH * g
        for t in range(3):
            at = start + PIECE * t
            tile = third[block:, at - at % LANES : at - at % LANES + LANES]
            tail_ref[pl.ds(t, rest, stride=3), :] = pltpu.roll(tile, (WIDTH - at) % LANES, 1)
        piece = third[:block, start : start + WIDTH]
        piece = jnp.concatenate([piece, jnp.zeros((block, PIECE), F32)], axis=1)
        out_ref[block * g : block * (g + 1), :] = jnp.where(lane < WIDTH, piece, tail_ref[...]).astype(BF16)


def arrival_order(owners):
    block = owners * MESSAGE
    comps = owners * COMPS
    table = np.zeros((ROWS * comps, ROWS * comps), np.float32)
    for owner in range(owners):
        for row in range(ROWS):
            for j in range(MAIN):
                table[row * comps + owner * COMPS + j, owner * MESSAGE + row * MAIN + j] = 1
            for i in range(2):
                table[row * comps + owner * COMPS + MAIN + i, block + owner * MAIN + row * 2 + i] = 1
    return table


def in_vmem(count):
    return [pl.BlockSpec(memory_space=pltpu.VMEM)] * count


def per_device(tiles, owners, field, norm_field, vertical, x_filter, y_filter):
    lines, comps, width = field.shape
    total = tiles * owners * MESSAGE
    params = pltpu.CompilerParams(vmem_limit_bytes=40 * 1024 * 1024)
    message_rows = jax.ShapeDtypeStruct((total, LANES), BF16)
    rows_scratch = pltpu.VMEM((total, LANES), F32)

    def exchange(rows):
        grouped = rows.reshape(tiles * owners, MESSAGE // 2, 2, LANES)
        moved = lax.all_to_all(grouped, ("gx", "gy"), split_axis=0, concat_axis=0, tiled=True)
        return moved.reshape(total, LANES)

    rows = pl.pallas_call(
        spread_kernel,
        out_shape=message_rows,
        in_specs=in_vmem(2),
        out_specs=pl.BlockSpec(memory_space=pltpu.VMEM),
        scratch_shapes=[rows_scratch],
        compiler_params=params,
        name="spread",
    )(jnp.transpose(field, (1, 2, 0)), y_filter)
    rows = exchange(rows)
    rows = pl.pallas_call(
        functools.partial(middle_kernel, tiles=tiles, owners=owners),
        out_shape=message_rows,
        in_specs=in_vmem(5),
        out_specs=pl.BlockSpec(memory_space=pltpu.VMEM),
        scratch_shapes=[rows_scratch, pltpu.VMEM((owners * MESSAGE, LANES), F32)],
        compiler_params=params,
        name="middle",
    )(rows, x_filter, norm_field, vertical, jnp.asarray(arrival_order(owners), BF16))
    rows = exchange(rows)
    result = pl.pallas_call(
        gather_kernel,
        out_shape=jax.ShapeDtypeStruct((comps, width, lines), BF16),
        in_specs=in_vmem(2),
        out_specs=pl.BlockSpec(memory_space=pltpu.VMEM),
        scratch_shapes=[rows_scratch],
        compiler_params=params,
        name="gather",
    )(rows, y_filter)
    return jnp.transpose(result, (2, 0, 1))


def solution(mesh):
    return jax.shard_map(
        functools.partial(per_device, mesh.shape["gx"], mesh.shape["gy"]),
        mesh=mesh,
        in_specs=(P(None, "gy", "gx"), P(("gx", "gy"), None, None), P(), P(), P()),
        out_specs=P(None, "gy", "gx"),
        check_vma=False,
    )
```

```python
import functools

import jax
import jax.numpy as jnp
import numpy as np
from jax import lax
from jax.experimental import pallas as pl
from jax.experimental.pallas import tpu as pltpu
from jax.sharding import PartitionSpec as P

LANES = 128
WIDTH = 96
PIECE = 32
MAIN = 6
ROWS = 3
COMPS = 8
MESSAGE = ROWS * MAIN
F32 = jnp.float32
BF16 = jnp.bfloat16


def dot(a, b, contract):
    return lax.dot_general(a, b, ((contract[:1], contract[1:]), ((), ())), preferred_element_type=F32)


def spread_kernel(field_ref, filter_ref, out_ref, rows_ref):
    lines = filter_ref.shape[0]
    parts = []
    for j in range(MAIN):
        start = PIECE * (j % 3)
        parts += [field_ref[j], field_ref[MAIN + j // 3, start : start + PIECE, :]]
    lines_in = jnp.concatenate(parts, axis=0)
    chunk = lines // 3
    for at in range(0, lines, chunk):
        first = dot(filter_ref[:, at : at + chunk], lines_in, (0, 1))
        for j in range(MAIN):
            rows_ref[pl.ds(MAIN * at + j, chunk, stride=MAIN), :] = first[:, j * LANES : (j + 1) * LANES]
        span = pl.ds(MAIN * at, MAIN * chunk)
        out_ref[span, :] = rows_ref[span, :].astype(BF16)


def gather_kernel(rows_in_ref, filter_ref, out_hbm, rows_ref, out_ref, sems):
    filt = filter_ref[...]
    lines = filt.shape[0]
    rows_ref[...] = rows_in_ref[...].astype(F32)
    stores = []
    for side in range(2):
        turned = []
        for j in range(3 * side, 3 * side + 3):
            turned.append(jnp.transpose(rows_ref[pl.ds(j, lines, stride=MAIN), :].astype(BF16)))
        result = dot(jnp.concatenate(turned, axis=0), filt, (1, 1)).astype(BF16)
        for t in range(3):
            out_ref[3 * side + t] = result[LANES * t : LANES * t + WIDTH]
            out_ref[MAIN + side, PIECE * t : PIECE * (t + 1), :] = result[LANES * t + WIDTH : LANES * (t + 1)]
        for n, span in enumerate((pl.ds(3 * side, 3), pl.ds(MAIN + side, 1))):
            stores.append(pltpu.make_async_copy(out_ref.at[span], out_hbm.at[span], sems.at[2 * side + n]))
            stores[-1].start()
    for store in stores:
        store.wait()


def middle_kernel(
    rows_in_ref, filter_ref, norm_ref, vertical_ref, order_ref, out_ref, rows_ref, tail_ref, *, tiles, owners
):
    weights = []
    for s in range(vertical_ref.shape[0]):
        factor = vertical_ref[s]
        weight = lax.dot_general(
            factor, factor, (((1,), (1,)), ((), ())), precision=lax.Precision.HIGHEST, preferred_element_type=F32
        )
        high = weight.astype(BF16)
        low = (weight - high.astype(F32)).astype(BF16)
        weights.append(jnp.concatenate([high, high, low], axis=1))
    filt = filter_ref[...]
    order = order_ref[...]
    block = owners * MESSAGE
    rest = block // 3
    rows_ref[...] = rows_in_ref[...].astype(F32)
    main = [rows_ref[block * g : block * (g + 1), :WIDTH] for g in range(tiles)]
    left = jnp.concatenate(main, axis=1).astype(BF16)
    tail = []
    for g in range(tiles):
        for t in range(3):
            tail.append(rows_ref[pl.ds(block * g + t, rest, stride=3), :][:, WIDTH:])
    below = jnp.concatenate(tail, axis=1).astype(BF16)
    lines = jnp.concatenate([left, below], axis=0)
    second = dot(lines, filt, (1, 0)).astype(BF16)
    second = dot(order, second, (1, 0))
    comps = norm_ref.shape[1]
    levels = vertical_ref.shape[1]
    raised = []
    for r in range(ROWS):
        for s in range(vertical_ref.shape[0]):
            span = slice(s * levels, (s + 1) * levels)
            scales = norm_ref[r, span, :]
            scaled = scales * second[r * comps + s * levels : r * comps + (s + 1) * levels]
            upper = scaled.astype(BF16)
            under = (scaled - upper.astype(F32)).astype(BF16)
            product = dot(weights[s], jnp.concatenate([upper, under, upper], axis=0), (1, 0))
            raised.append((scales * product).astype(BF16))
    middle = jnp.concatenate(raised, axis=0)
    middle = dot(order, middle, (0, 0)).astype(BF16)
    third = dot(middle, filt, (1, 1))
    lane = lax.broadcasted_iota(jnp.int32, (block, LANES), 1)
    for g in range(tiles):
        start = WIDTH * g
        for t in range(3):
            at = start + PIECE * t
            tile = third[block:, at - at % LANES : at - at % LANES + LANES]
            tail_ref[pl.ds(t, rest, stride=3), :] = pltpu.roll(tile, (WIDTH - at) % LANES, 1)
        piece = third[:block, start : start + WIDTH]
        piece = jnp.concatenate([piece, jnp.zeros((block, PIECE), F32)], axis=1)
        out_ref[block * g : block * (g + 1), :] = jnp.where(lane < WIDTH, piece, tail_ref[...]).astype(BF16)


def arrival_order(owners):
    block = owners * MESSAGE
    comps = owners * COMPS
    table = np.zeros((ROWS * comps, ROWS * comps), np.float32)
    for owner in range(owners):
        for row in range(ROWS):
            for j in range(MAIN):
                table[row * comps + owner * COMPS + j, owner * MESSAGE + row * MAIN + j] = 1
            for i in range(2):
                table[row * comps + owner * COMPS + MAIN + i, block + owner * MAIN + row * 2 + i] = 1
    return table


VMEM = pl.BlockSpec(memory_space=pltpu.VMEM)
HBM = pl.BlockSpec(memory_space=pltpu.HBM)
SPREAD_FLOPS = 2 * 10**10


def per_device(tiles, owners, field, norm_field, vertical, x_filter, y_filter):
    lines, comps, width = field.shape
    total = tiles * owners * MESSAGE
    message_rows = jax.ShapeDtypeStruct((total, LANES), BF16)
    rows_scratch = pltpu.VMEM((total, LANES), F32)
    field_scratch = pltpu.VMEM((comps, width, lines), BF16)
    sems = pltpu.SemaphoreType.DMA

    def call(kernel, name, out_shape, in_specs, out_specs, scratch, *operands, flops):
        return pl.pallas_call(
            kernel,
            out_shape=out_shape,
            in_specs=in_specs,
            out_specs=out_specs,
            scratch_shapes=scratch,
            compiler_params=pltpu.CompilerParams(vmem_limit_bytes=40 * 1024 * 1024),
            cost_estimate=pl.CostEstimate(flops=flops, bytes_accessed=sum(a.nbytes for a in operands), transcendentals=0),
            name=name,
        )(*operands)

    def exchange(rows):
        grouped = rows.reshape(tiles * owners, MESSAGE // 2, 2, LANES)
        moved = lax.all_to_all(grouped, ("gx", "gy"), split_axis=0, concat_axis=0, tiled=True)
        return moved.reshape(total, LANES)

    own = jnp.transpose(field, (1, 2, 0))
    rows = call(spread_kernel, "spread", message_rows, [VMEM, VMEM], VMEM, [rows_scratch], own, y_filter, flops=SPREAD_FLOPS)
    rows = exchange(rows)
    scratch = [rows_scratch, pltpu.VMEM((owners * MESSAGE, LANES), F32)]
    middle = functools.partial(middle_kernel, tiles=tiles, owners=owners)
    order = jnp.asarray(arrival_order(owners), BF16)
    rows = call(middle, "middle", message_rows, [VMEM] * 5, VMEM, scratch, rows, x_filter, norm_field, vertical, order, flops=5 * 10**9)
    rows = exchange(rows)
    result = jax.ShapeDtypeStruct((comps, width, lines), BF16)
    result = call(gather_kernel, "gather", result, [VMEM, VMEM], HBM, [rows_scratch, field_scratch, sems((4,))], rows, y_filter, flops=10**9)
    return jnp.transpose(result, (2, 0, 1))


def solution(mesh):
    return jax.shard_map(
        functools.partial(per_device, mesh.shape["gx"], mesh.shape["gy"]),
        mesh=mesh,
        in_specs=(P(None, "gy", "gx"), P(("gx", "gy"), None, None), P(), P(), P()),
        out_specs=P(None, "gy", "gx"),
        check_vma=False,
    )
```

```python
import functools

import jax
import jax.numpy as jnp
import numpy as np
from jax import lax
from jax.experimental import pallas as pl
from jax.experimental.pallas import tpu as pltpu
from jax.sharding import PartitionSpec as P

LANES = 128
WIDTH = 96
PIECE = 32
MAIN = 6
ROWS = 3
COMPS = 8
MESSAGE = ROWS * MAIN
F32 = jnp.float32
BF16 = jnp.bfloat16


def dot(a, b, contract):
    return lax.dot_general(a, b, ((contract[:1], contract[1:]), ((), ())), preferred_element_type=F32)


def level_weight(vertical_ref):
    size = vertical_ref.shape[0] * vertical_ref.shape[1]
    rows = []
    for s in range(vertical_ref.shape[0]):
        factor = vertical_ref[s]
        weight = lax.dot_general(
            factor, factor, (((1,), (1,)), ((), ())), precision=lax.Precision.HIGHEST, preferred_element_type=F32
        )
        blank = jnp.zeros_like(weight)
        rows.append(jnp.concatenate([weight if n == s else blank for n in range(size // weight.shape[0])], axis=1))
    full = jnp.concatenate(rows, axis=0)
    high = full.astype(BF16)
    low = (full - high.astype(F32)).astype(BF16)
    return jnp.concatenate([high, high, low], axis=1)


def spread_kernel(
    field_hbm, filter_hbm, vertical_hbm, out_ref, weight_ref, field_ref, filter_ref, vertical_ref, rows_ref, sems
):
    pairs = ((vertical_hbm, vertical_ref), (field_hbm, field_ref), (filter_hbm, filter_ref))
    loads = [pltpu.make_async_copy(source, target, sems.at[n]) for n, (source, target) in enumerate(pairs)]
    for load in loads:
        load.start()
    loads[0].wait()
    weight_ref[...] = level_weight(vertical_ref)
    for load in loads[1:]:
        load.wait()
    lines = filter_ref.shape[0]
    parts = []
    for j in range(MAIN):
        start = PIECE * (j % 3)
        parts += [field_ref[j], field_ref[MAIN + j // 3, start : start + PIECE, :]]
    lines_in = jnp.concatenate(parts, axis=0)
    chunk = lines // 3
    for at in range(0, lines, chunk):
        first = dot(filter_ref[:, at : at + chunk], lines_in, (0, 1))
        for j in range(MAIN):
            rows_ref[pl.ds(MAIN * at + j, chunk, stride=MAIN), :] = first[:, j * LANES : (j + 1) * LANES]
        span = pl.ds(MAIN * at, MAIN * chunk)
        out_ref[span, :] = rows_ref[span, :].astype(BF16)


def gather_kernel(rows_in_ref, filter_ref, out_hbm, rows_ref, out_ref, sems):
    filt = filter_ref[...]
    lines = filt.shape[0]
    rows_ref[...] = rows_in_ref[...].astype(F32)
    stores = []
    for side in range(2):
        turned = []
        for j in range(3 * side, 3 * side + 3):
            turned.append(jnp.transpose(rows_ref[pl.ds(j, lines, stride=MAIN), :].astype(BF16)))
        result = dot(jnp.concatenate(turned, axis=0), filt, (1, 1)).astype(BF16)
        for t in range(3):
            out_ref[3 * side + t] = result[LANES * t : LANES * t + WIDTH]
            out_ref[MAIN + side, PIECE * t : PIECE * (t + 1), :] = result[LANES * t + WIDTH : LANES * (t + 1)]
        for n, span in enumerate((pl.ds(3 * side, 3), pl.ds(MAIN + side, 1))):
            stores.append(pltpu.make_async_copy(out_ref.at[span], out_hbm.at[span], sems.at[2 * side + n]))
            stores[-1].start()
    for store in stores:
        store.wait()


def middle_kernel(
    rows_in_ref, filter_ref, norm_ref, weight_ref, order_ref, out_ref, rows_ref, tail_ref, *, tiles, owners
):
    filt = filter_ref[...]
    order = order_ref[...]
    block = owners * MESSAGE
    rest = block // 3
    rows_ref[...] = rows_in_ref[...].astype(F32)
    main = [rows_ref[block * g : block * (g + 1), :WIDTH] for g in range(tiles)]
    left = jnp.concatenate(main, axis=1).astype(BF16)
    tail = []
    for g in range(tiles):
        for t in range(3):
            tail.append(rows_ref[pl.ds(block * g + t, rest, stride=3), :][:, WIDTH:])
    below = jnp.concatenate(tail, axis=1).astype(BF16)
    lines = jnp.concatenate([left, below], axis=0)
    second = dot(lines, filt, (1, 0)).astype(BF16)
    second = dot(order, second, (1, 0))
    comps = norm_ref.shape[1]
    raised = []
    for r in range(ROWS):
        scales = norm_ref[r]
        scaled = scales * second[r * comps : (r + 1) * comps]
        upper = scaled.astype(BF16)
        under = (scaled - upper.astype(F32)).astype(BF16)
        product = dot(weight_ref[...], jnp.concatenate([upper, under, upper], axis=0), (1, 0))
        raised.append((scales * product).astype(BF16))
    middle = jnp.concatenate(raised, axis=0)
    middle = dot(order, middle, (0, 0)).astype(BF16)
    lane = lax.broadcasted_iota(jnp.int32, (block, LANES), 1)
    half = tiles // 2
    for g in range(tiles):
        if g % half == 0:
            third = dot(middle, filt[WIDTH * g : WIDTH * (g + half)], (1, 1))
        start = WIDTH * (g % half)
        for t in range(3):
            at = start + PIECE * t
            tile = third[block:, at - at % LANES : at - at % LANES + LANES]
            tail_ref[pl.ds(t, rest, stride=3), :] = pltpu.roll(tile, (WIDTH - at) % LANES, 1)
        piece = third[:block, start : start + WIDTH]
        piece = jnp.concatenate([piece, jnp.zeros((block, PIECE), F32)], axis=1)
        out_ref[block * g : block * (g + 1), :] = jnp.where(lane < WIDTH, piece, tail_ref[...]).astype(BF16)


def arrival_order(owners):
    block = owners * MESSAGE
    comps = owners * COMPS
    table = np.zeros((ROWS * comps, ROWS * comps), np.float32)
    for owner in range(owners):
        for row in range(ROWS):
            for j in range(MAIN):
                table[row * comps + owner * COMPS + j, owner * MESSAGE + row * MAIN + j] = 1
            for i in range(2):
                table[row * comps + owner * COMPS + MAIN + i, block + owner * MAIN + row * 2 + i] = 1
    return table


VMEM = pl.BlockSpec(memory_space=pltpu.VMEM)
HBM = pl.BlockSpec(memory_space=pltpu.HBM)
SPREAD_FLOPS = 2 * 10**10


def per_device(tiles, owners, field, norm_field, vertical, x_filter, y_filter):
    lines, comps, width = field.shape
    total = tiles * owners * MESSAGE
    message_rows = jax.ShapeDtypeStruct((total, LANES), BF16)
    rows_scratch = pltpu.VMEM((total, LANES), F32)
    field_scratch = pltpu.VMEM((comps, width, lines), BF16)
    sems = pltpu.SemaphoreType.DMA

    def call(kernel, name, out_shape, in_specs, out_specs, scratch, *operands, flops):
        return pl.pallas_call(
            kernel,
            out_shape=out_shape,
            in_specs=in_specs,
            out_specs=out_specs,
            scratch_shapes=scratch,
            compiler_params=pltpu.CompilerParams(vmem_limit_bytes=40 * 1024 * 1024),
            cost_estimate=pl.CostEstimate(flops=flops, bytes_accessed=sum(a.nbytes for a in operands), transcendentals=0),
            name=name,
        )(*operands)

    def exchange(rows):
        grouped = rows.reshape(tiles * owners, MESSAGE // 2, 2, LANES)
        moved = lax.all_to_all(grouped, ("gx", "gy"), split_axis=0, concat_axis=0, tiled=True)
        return moved.reshape(total, LANES)

    def in_hbm(array):
        return pltpu.with_memory_space_constraint(array, pltpu.HBM)

    levels = vertical.shape[0] * vertical.shape[1]
    weight = jax.ShapeDtypeStruct((levels, 3 * levels), BF16)
    scratch = [field_scratch] + [pltpu.VMEM(a.shape, a.dtype) for a in (y_filter, vertical)] + [rows_scratch, sems((3,))]
    operands = [in_hbm(a) for a in (jnp.transpose(field, (1, 2, 0)), y_filter, vertical)]
    out = (message_rows, weight)
    rows, weight = call(spread_kernel, "spread", out, [HBM] * 3, (VMEM, VMEM), scratch, *operands, flops=SPREAD_FLOPS)
    rows = exchange(rows)
    scratch = [rows_scratch, pltpu.VMEM((owners * MESSAGE, LANES), F32)]
    middle = functools.partial(middle_kernel, tiles=tiles, owners=owners)
    order = jnp.asarray(arrival_order(owners), BF16)
    rows = call(middle, "middle", message_rows, [VMEM] * 5, VMEM, scratch, rows, x_filter, norm_field, weight, order, flops=5 * 10**9)
    rows = exchange(rows)
    result = jax.ShapeDtypeStruct((comps, width, lines), BF16)
    result = call(gather_kernel, "gather", result, [VMEM, VMEM], HBM, [rows_scratch, field_scratch, sems((4,))], rows, y_filter, flops=10**9)
    return jnp.transpose(result, (2, 0, 1))


def solution(mesh):
    return jax.shard_map(
        functools.partial(per_device, mesh.shape["gx"], mesh.shape["gy"]),
        mesh=mesh,
        in_specs=(P(None, "gy", "gx"), P(("gx", "gy"), None, None), P(), P(), P()),
        out_specs=P(None, "gy", "gx"),
        check_vma=False,
    )
```

```python
import functools

import jax
import jax.numpy as jnp
from jax import lax
from jax.experimental import pallas as pl
from jax.experimental.pallas import tpu as pltpu
from jax.sharding import PartitionSpec as P

LANES = 128
WIDTH = 96
PIECE = 32
MAIN = 6
ROWS = 3
COMPS = 8
MESSAGE = ROWS * MAIN
F32 = jnp.float32
BF16 = jnp.bfloat16


def dot(a, b, contract):
    return lax.dot_general(a, b, ((contract[:1], contract[1:]), ((), ())), preferred_element_type=F32)


def level_weight(vertical_ref):
    size = vertical_ref.shape[0] * vertical_ref.shape[1]
    rows = []
    for s in range(vertical_ref.shape[0]):
        factor = vertical_ref[s]
        weight = lax.dot_general(
            factor, factor, (((1,), (1,)), ((), ())), precision=lax.Precision.HIGHEST, preferred_element_type=F32
        )
        blank = jnp.zeros_like(weight)
        rows.append(jnp.concatenate([weight if n == s else blank for n in range(size // weight.shape[0])], axis=1))
    full = jnp.concatenate(rows, axis=0)
    high = full.astype(BF16)
    low = (full - high.astype(F32)).astype(BF16)
    owners = size // COMPS
    row = lax.broadcasted_iota(jnp.int32, (size, size), 0)
    col = lax.broadcasted_iota(jnp.int32, (size, size), 1)
    order = (COMPS * (row % owners) + row // owners == col).astype(BF16)
    high, low = (dot(dot(order, part, (1, 0)).astype(BF16), order, (1, 1)).astype(BF16) for part in (high, low))
    return jnp.concatenate([high, high, low], axis=1)


def spread_kernel(
    field_hbm, filter_hbm, vertical_hbm, out_ref, weight_ref, field_ref, filter_ref, vertical_ref, rows_ref, sems
):
    pairs = ((vertical_hbm, vertical_ref), (field_hbm, field_ref), (filter_hbm, filter_ref))
    loads = [pltpu.make_async_copy(source, target, sems.at[n]) for n, (source, target) in enumerate(pairs)]
    for load in loads:
        load.start()
    loads[0].wait()
    weight_ref[...] = level_weight(vertical_ref)
    for load in loads[1:]:
        load.wait()
    lines = filter_ref.shape[0]
    parts = []
    for j in range(MAIN):
        start = PIECE * (j % 3)
        parts += [field_ref[j], field_ref[MAIN + j // 3, start : start + PIECE, :]]
    lines_in = jnp.concatenate(parts, axis=0)
    chunk = lines // 3
    for at in range(0, lines, chunk):
        first = dot(filter_ref[:, at : at + chunk], lines_in, (0, 1))
        for j in range(MAIN):
            rows_ref[pl.ds(MAIN * at + j, chunk, stride=MAIN), :] = first[:, j * LANES : (j + 1) * LANES]
        span = pl.ds(MAIN * at, MAIN * chunk)
        out_ref[span, :] = rows_ref[span, :].astype(BF16)


def gather_kernel(rows_in_ref, filter_ref, out_hbm, rows_ref, out_ref, sems):
    filt = filter_ref[...]
    lines = filt.shape[0]
    rows_ref[...] = rows_in_ref[...].astype(F32)
    stores = []
    for side in range(2):
        turned = []
        for j in range(3 * side, 3 * side + 3):
            turned.append(jnp.transpose(rows_ref[pl.ds(j, lines, stride=MAIN), :].astype(BF16)))
        result = dot(jnp.concatenate(turned, axis=0), filt, (1, 1)).astype(BF16)
        for t in range(3):
            out_ref[3 * side + t] = result[LANES * t : LANES * t + WIDTH]
            out_ref[MAIN + side, PIECE * t : PIECE * (t + 1), :] = result[LANES * t + WIDTH : LANES * (t + 1)]
        for n, span in enumerate((pl.ds(3 * side, 3), pl.ds(MAIN + side, 1))):
            stores.append(pltpu.make_async_copy(out_ref.at[span], out_hbm.at[span], sems.at[2 * side + n]))
            stores[-1].start()
    for store in stores:
        store.wait()


def middle_kernel(
    rows_in_ref, filter_ref, norm_ref, weight_ref, out_ref, rows_ref, stage_ref, tiled_ref, *, tiles, owners
):
    blocks = tiled_ref.shape[0]
    for n in range(blocks):
        tiled_ref[n] = norm_ref[:, :, LANES * n : LANES * (n + 1)]
    block = owners * MESSAGE
    rows_ref[...] = rows_in_ref[...].astype(F32)

    def arrived(g, r, j):
        return rows_ref[pl.ds(block * g + MAIN * r + j, owners, stride=MESSAGE), :]

    def scales(r):
        parts = []
        for c in range(COMPS):
            pieces = [tiled_ref.at[n, r][pl.ds(c, owners, stride=COMPS), :] for n in range(blocks)]
            parts.append(jnp.concatenate(pieces, axis=1))
        return jnp.concatenate(parts, axis=0)

    lines = []
    for r in range(ROWS):
        rows = [[arrived(g, r, j) for j in range(MAIN)] for g in range(tiles)]
        for j in range(MAIN):
            lines.append(jnp.concatenate([row[j][:, :WIDTH] for row in rows], axis=1).astype(BF16))
        for i in range(2):
            pieces = [row[3 * i + t][:, WIDTH:] for row in rows for t in range(3)]
            lines.append(jnp.concatenate(pieces, axis=1).astype(BF16))
    filt = filter_ref[...]
    second = dot(jnp.concatenate(lines, axis=0), filt, (1, 0)).astype(BF16).astype(F32)
    comps = owners * COMPS
    raised = []
    for r in range(ROWS):
        scaled = scales(r) * second[r * comps : (r + 1) * comps]
        upper = scaled.astype(BF16)
        under = (scaled - upper.astype(F32)).astype(BF16)
        product = dot(weight_ref[...], jnp.concatenate([upper, under, upper], axis=0), (1, 0))
        raised.append((scales(r) * product).astype(BF16))
    middle = jnp.concatenate(raised, axis=0)
    lane = lax.broadcasted_iota(jnp.int32, (owners, LANES), 1)
    half = tiles // 2
    for g in range(tiles):
        if g % half == 0:
            third = dot(middle, filt[WIDTH * g : WIDTH * (g + half)], (1, 1))
        start = WIDTH * (g % half)
        for r in range(ROWS):
            for j in range(MAIN):
                line = r * comps + j * owners
                piece = third[line : line + owners, start : start + WIDTH]
                piece = jnp.concatenate([piece, jnp.zeros((owners, PIECE), F32)], axis=1)
                line = r * comps + (MAIN + j // 3) * owners
                at = start + PIECE * (j % 3)
                tile = third[line : line + owners, at - at % LANES : at - at % LANES + LANES]
                tile = pltpu.roll(tile, (WIDTH - at) % LANES, 1)
                stage_ref[pl.ds(MAIN * r + j, owners, stride=MESSAGE), :] = jnp.where(lane < WIDTH, piece, tile)
        out_ref[block * g : block * (g + 1), :] = stage_ref[...].astype(BF16)


VMEM = pl.BlockSpec(memory_space=pltpu.VMEM)
HBM = pl.BlockSpec(memory_space=pltpu.HBM)
SPREAD_FLOPS = 2 * 10**10


def per_device(tiles, owners, field, norm_field, vertical, x_filter, y_filter):
    lines, comps, width = field.shape
    total = tiles * owners * MESSAGE
    message_rows = jax.ShapeDtypeStruct((total, LANES), BF16)
    rows_scratch = pltpu.VMEM((total, LANES), F32)
    field_scratch = pltpu.VMEM((comps, width, lines), BF16)
    sems = pltpu.SemaphoreType.DMA

    def call(kernel, name, out_shape, in_specs, out_specs, scratch, *operands, flops):
        return pl.pallas_call(
            kernel,
            out_shape=out_shape,
            in_specs=in_specs,
            out_specs=out_specs,
            scratch_shapes=scratch,
            compiler_params=pltpu.CompilerParams(vmem_limit_bytes=40 * 1024 * 1024),
            cost_estimate=pl.CostEstimate(flops=flops, bytes_accessed=sum(a.nbytes for a in operands), transcendentals=0),
            name=name,
        )(*operands)

    def exchange(rows):
        grouped = rows.reshape(tiles * owners, MESSAGE // 2, 2, LANES)
        moved = lax.all_to_all(grouped, ("gx", "gy"), split_axis=0, concat_axis=0, tiled=True)
        return moved.reshape(total, LANES)

    def in_hbm(array):
        return pltpu.with_memory_space_constraint(array, pltpu.HBM)

    levels = vertical.shape[0] * vertical.shape[1]
    weight = jax.ShapeDtypeStruct((levels, 3 * levels), BF16)
    scratch = [field_scratch] + [pltpu.VMEM(a.shape, a.dtype) for a in (y_filter, vertical)] + [rows_scratch, sems((3,))]
    operands = [in_hbm(a) for a in (jnp.transpose(field, (1, 2, 0)), y_filter, vertical)]
    out = (message_rows, weight)
    rows, weight = call(spread_kernel, "spread", out, [HBM] * 3, (VMEM, VMEM), scratch, *operands, flops=SPREAD_FLOPS)
    rows = exchange(rows)
    blocks = x_filter.shape[0] // LANES
    norm_scratch = pltpu.VMEM((blocks, ROWS, levels, LANES), F32)
    scratch = [rows_scratch, pltpu.VMEM((owners * MESSAGE, LANES), F32), norm_scratch]
    middle = functools.partial(middle_kernel, tiles=tiles, owners=owners)
    operands = (rows, x_filter, norm_field, weight)
    rows = call(middle, "middle", message_rows, [VMEM] * 4, VMEM, scratch, *operands, flops=5 * 10**9)
    rows = exchange(rows)
    result = jax.ShapeDtypeStruct((comps, width, lines), BF16)
    result = call(gather_kernel, "gather", result, [VMEM, VMEM], HBM, [rows_scratch, field_scratch, sems((4,))], rows, y_filter, flops=10**9)
    return jnp.transpose(result, (2, 0, 1))


def solution(mesh):
    return jax.shard_map(
        functools.partial(per_device, mesh.shape["gx"], mesh.shape["gy"]),
        mesh=mesh,
        in_specs=(P(None, "gy", "gx"), P(("gx", "gy"), None, None), P(), P(), P()),
        out_specs=P(None, "gy", "gx"),
        check_vma=False,
    )
```

```python
import functools

import jax
import jax.numpy as jnp
from jax import lax
from jax.experimental import pallas as pl
from jax.experimental.pallas import tpu as pltpu
from jax.sharding import PartitionSpec as P

LANES = 128
WIDTH = 96
PIECE = 32
MAIN = 6
ROWS = 3
COMPS = 8
MESSAGE = ROWS * MAIN
F32 = jnp.float32
BF16 = jnp.bfloat16


def dot(a, b, contract):
    return lax.dot_general(a, b, ((contract[:1], contract[1:]), ((), ())), preferred_element_type=F32)


def level_weight(vertical_ref):
    size = vertical_ref.shape[0] * vertical_ref.shape[1]
    rows = []
    for s in range(vertical_ref.shape[0]):
        factor = vertical_ref[s]
        weight = lax.dot_general(
            factor, factor, (((1,), (1,)), ((), ())), precision=lax.Precision.HIGHEST, preferred_element_type=F32
        )
        blank = jnp.zeros_like(weight)
        rows.append(jnp.concatenate([weight if n == s else blank for n in range(size // weight.shape[0])], axis=1))
    full = jnp.concatenate(rows, axis=0)
    high = full.astype(BF16)
    low = (full - high.astype(F32)).astype(BF16)
    owners = size // COMPS
    row = lax.broadcasted_iota(jnp.int32, (size, size), 0)
    col = lax.broadcasted_iota(jnp.int32, (size, size), 1)
    order = (COMPS * (row % owners) + row // owners == col).astype(BF16)
    high, low = (dot(dot(order, part, (1, 0)).astype(BF16), order, (1, 1)).astype(BF16) for part in (high, low))
    return jnp.concatenate([high, high, low], axis=1)


def spread_kernel(
    field_hbm, filter_hbm, vertical_hbm, out_ref, weight_ref, field_ref, filter_ref, vertical_ref, rows_ref, sems
):
    pairs = ((field_hbm, field_ref), (filter_hbm, filter_ref), (vertical_hbm, vertical_ref))
    loads = [pltpu.make_async_copy(source, target, sems.at[n]) for n, (source, target) in enumerate(pairs)]
    for load in loads:
        load.start()
    loads[2].wait()
    weight_ref[...] = level_weight(vertical_ref)
    for load in loads[:2]:
        load.wait()
    lines = filter_ref.shape[0]
    parts = []
    for j in range(MAIN):
        start = PIECE * (j % 3)
        parts += [field_ref[j], field_ref[MAIN + j // 3, start : start + PIECE, :]]
    lines_in = jnp.concatenate(parts, axis=0)
    chunk = lines // 3
    for at in range(0, lines, chunk):
        first = dot(filter_ref[:, at : at + chunk], lines_in, (0, 1))
        for j in range(MAIN):
            rows_ref[pl.ds(MAIN * at + j, chunk, stride=MAIN), :] = first[:, j * LANES : (j + 1) * LANES]
        span = pl.ds(MAIN * at, MAIN * chunk)
        out_ref[span, :] = rows_ref[span, :].astype(BF16)


def gather_kernel(rows_in_ref, filter_ref, out_hbm, rows_ref, out_ref, sems):
    filt = filter_ref[...]
    lines = filt.shape[0]
    rows_ref[...] = rows_in_ref[...].astype(F32)
    stores = []
    for side in range(2):
        turned = []
        for j in range(3 * side, 3 * side + 3):
            turned.append(jnp.transpose(rows_ref[pl.ds(j, lines, stride=MAIN), :].astype(BF16)))
        result = dot(jnp.concatenate(turned, axis=0), filt, (1, 1)).astype(BF16)
        for t in range(3):
            out_ref[3 * side + t] = result[LANES * t : LANES * t + WIDTH]
            out_ref[MAIN + side, PIECE * t : PIECE * (t + 1), :] = result[LANES * t + WIDTH : LANES * (t + 1)]
        for n, span in enumerate((pl.ds(3 * side, 3), pl.ds(MAIN + side, 1))):
            stores.append(pltpu.make_async_copy(out_ref.at[span], out_hbm.at[span], sems.at[2 * side + n]))
            stores[-1].start()
    for store in stores:
        store.wait()


def middle_kernel(
    rows_in_ref, filter_ref, norm_ref, weight_ref, out_ref, rows_ref, stage_ref, tiled_ref, *, tiles, owners
):
    blocks = tiled_ref.shape[0]
    for n in range(blocks):
        tiled_ref[n] = norm_ref[:, :, LANES * n : LANES * (n + 1)]
    block = owners * MESSAGE
    rows_ref[...] = rows_in_ref[...].astype(F32)

    def arrived(g, r, j):
        return rows_ref[pl.ds(block * g + MAIN * r + j, owners, stride=MESSAGE), :]

    def scales(r):
        parts = []
        for c in range(COMPS):
            pieces = [tiled_ref.at[n, r][pl.ds(c, owners, stride=COMPS), :] for n in range(blocks)]
            parts.append(jnp.concatenate(pieces, axis=1))
        return jnp.concatenate(parts, axis=0)

    lines = []
    for r in range(ROWS):
        rows = [[arrived(g, r, j) for j in range(MAIN)] for g in range(tiles)]
        for j in range(MAIN):
            lines.append(jnp.concatenate([row[j][:, :WIDTH] for row in rows], axis=1).astype(BF16))
        for i in range(2):
            pieces = [row[3 * i + t][:, WIDTH:] for row in rows for t in range(3)]
            lines.append(jnp.concatenate(pieces, axis=1).astype(BF16))
    filt = filter_ref[...]
    second = dot(jnp.concatenate(lines, axis=0), filt, (1, 0)).astype(BF16).astype(F32)
    comps = owners * COMPS
    raised = []
    for r in range(ROWS):
        scaled = scales(r) * second[r * comps : (r + 1) * comps]
        upper = scaled.astype(BF16)
        under = (scaled - upper.astype(F32)).astype(BF16)
        product = dot(weight_ref[...], jnp.concatenate([upper, under, upper], axis=0), (1, 0))
        raised.append((scales(r) * product).astype(BF16))
    middle = jnp.concatenate(raised, axis=0)
    lane = lax.broadcasted_iota(jnp.int32, (owners, LANES), 1)
    half = tiles // 2
    for g in range(tiles):
        if g % half == 0:
            third = dot(middle, filt[WIDTH * g : WIDTH * (g + half)], (1, 1))
        start = WIDTH * (g % half)
        for r in range(ROWS):
            for j in range(MAIN):
                line = r * comps + j * owners
                piece = third[line : line + owners, start : start + WIDTH]
                piece = jnp.concatenate([piece, jnp.zeros((owners, PIECE), F32)], axis=1)
                line = r * comps + (MAIN + j // 3) * owners
                at = start + PIECE * (j % 3)
                tile = third[line : line + owners, at - at % LANES : at - at % LANES + LANES]
                tile = pltpu.roll(tile, (WIDTH - at) % LANES, 1)
                stage_ref[pl.ds(MAIN * r + j, owners, stride=MESSAGE), :] = jnp.where(lane < WIDTH, piece, tile)
        out_ref[block * g : block * (g + 1), :] = stage_ref[...].astype(BF16)


VMEM = pl.BlockSpec(memory_space=pltpu.VMEM)
HBM = pl.BlockSpec(memory_space=pltpu.HBM)
SPREAD_FLOPS = 2 * 10**10


def per_device(tiles, owners, field, norm_field, vertical, x_filter, y_filter):
    lines, comps, width = field.shape
    total = tiles * owners * MESSAGE
    message_rows = jax.ShapeDtypeStruct((total, LANES), BF16)
    rows_scratch = pltpu.VMEM((total, LANES), F32)
    field_scratch = pltpu.VMEM((comps, width, lines), BF16)
    sems = pltpu.SemaphoreType.DMA

    def call(kernel, name, out_shape, in_specs, out_specs, scratch, *operands, flops):
        return pl.pallas_call(
            kernel,
            out_shape=out_shape,
            in_specs=in_specs,
            out_specs=out_specs,
            scratch_shapes=scratch,
            compiler_params=pltpu.CompilerParams(vmem_limit_bytes=40 * 1024 * 1024),
            cost_estimate=pl.CostEstimate(flops=flops, bytes_accessed=sum(a.nbytes for a in operands), transcendentals=0),
            name=name,
        )(*operands)

    def exchange(rows):
        grouped = rows.reshape(tiles * owners, MESSAGE // 2, 2, LANES)
        moved = lax.all_to_all(grouped, ("gx", "gy"), split_axis=0, concat_axis=0, tiled=True)
        return moved.reshape(total, LANES)

    def in_hbm(array):
        return pltpu.with_memory_space_constraint(array, pltpu.HBM)

    levels = vertical.shape[0] * vertical.shape[1]
    weight = jax.ShapeDtypeStruct((levels, 3 * levels), BF16)
    scratch = [field_scratch] + [pltpu.VMEM(a.shape, a.dtype) for a in (y_filter, vertical)] + [rows_scratch, sems((3,))]
    operands = [in_hbm(a) for a in (jnp.transpose(field, (1, 2, 0)), y_filter, vertical)]
    out = (message_rows, weight)
    rows, weight = call(spread_kernel, "spread", out, [HBM] * 3, (VMEM, VMEM), scratch, *operands, flops=SPREAD_FLOPS)
    rows = exchange(rows)
    blocks = x_filter.shape[0] // LANES
    norm_scratch = pltpu.VMEM((blocks, ROWS, levels, LANES), F32)
    scratch = [rows_scratch, pltpu.VMEM((owners * MESSAGE, LANES), F32), norm_scratch]
    middle = functools.partial(middle_kernel, tiles=tiles, owners=owners)
    operands = (rows, x_filter, norm_field, weight)
    rows = call(middle, "middle", message_rows, [VMEM] * 4, VMEM, scratch, *operands, flops=5 * 10**9)
    rows = exchange(rows)
    result = jax.ShapeDtypeStruct((comps, width, lines), BF16)
    result = call(gather_kernel, "gather", result, [VMEM, VMEM], HBM, [rows_scratch, field_scratch, sems((4,))], rows, y_filter, flops=10**9)
    return jnp.transpose(result, (2, 0, 1))


def solution(mesh):
    return jax.shard_map(
        functools.partial(per_device, mesh.shape["gx"], mesh.shape["gy"]),
        mesh=mesh,
        in_specs=(P(None, "gy", "gx"), P(("gx", "gy"), None, None), P(), P(), P()),
        out_specs=P(None, "gy", "gx"),
        check_vma=False,
    )
```

```python
import functools

import jax
import jax.numpy as jnp
from jax import lax
from jax.experimental import pallas as pl
from jax.experimental.pallas import tpu as pltpu
from jax.sharding import PartitionSpec as P

LANES = 128
WIDTH = 96
PIECE = 32
MAIN = 6
ROWS = 3
COMPS = 8
MESSAGE = ROWS * MAIN
F32 = jnp.float32
BF16 = jnp.bfloat16


def dot(a, b, contract):
    return lax.dot_general(a, b, ((contract[:1], contract[1:]), ((), ())), preferred_element_type=F32)


def level_weight(vertical_ref):
    size = vertical_ref.shape[0] * vertical_ref.shape[1]
    rows = []
    for s in range(vertical_ref.shape[0]):
        factor = vertical_ref[s]
        weight = lax.dot_general(
            factor, factor, (((1,), (1,)), ((), ())), precision=lax.Precision.HIGHEST, preferred_element_type=F32
        )
        blank = jnp.zeros_like(weight)
        rows.append(jnp.concatenate([weight if n == s else blank for n in range(size // weight.shape[0])], axis=1))
    full = jnp.concatenate(rows, axis=0)
    high = full.astype(BF16)
    low = (full - high.astype(F32)).astype(BF16)
    owners = size // COMPS
    row = lax.broadcasted_iota(jnp.int32, (size, size), 0)
    col = lax.broadcasted_iota(jnp.int32, (size, size), 1)
    order = (COMPS * (row % owners) + row // owners == col).astype(BF16)
    high, low = (dot(dot(order, part, (1, 0)).astype(BF16), order, (1, 1)).astype(BF16) for part in (high, low))
    return jnp.concatenate([high, high, low], axis=1)


def spread_kernel(
    field_hbm, filter_hbm, vertical_hbm, out_ref, weight_ref, field_ref, filter_ref, vertical_ref, rows_ref, sems
):
    pairs = ((vertical_hbm, vertical_ref), (field_hbm, field_ref), (filter_hbm, filter_ref))
    loads = [pltpu.make_async_copy(source, target, sems.at[n]) for n, (source, target) in enumerate(pairs)]
    for load in loads:
        load.start()
    loads[0].wait()
    weight_ref[...] = level_weight(vertical_ref)
    for load in loads[1:]:
        load.wait()
    lines = filter_ref.shape[0]
    parts = []
    for j in range(MAIN):
        start = PIECE * (j % 3)
        parts += [field_ref[j], field_ref[MAIN + j // 3, start : start + PIECE, :]]
    lines_in = jnp.concatenate(parts, axis=0)
    chunk = lines // 3
    for at in range(0, lines, chunk):
        first = dot(filter_ref[:, at : at + chunk], lines_in, (0, 1))
        for j in range(MAIN):
            rows_ref[pl.ds(MAIN * at + j, chunk, stride=MAIN), :] = first[:, j * LANES : (j + 1) * LANES]
        span = pl.ds(MAIN * at, MAIN * chunk)
        out_ref[span, :] = rows_ref[span, :].astype(BF16)


def gather_kernel(rows_in_ref, filter_ref, out_hbm, rows_ref, out_ref, sems):
    filt = filter_ref[...]
    lines = filt.shape[0]
    rows_ref[...] = rows_in_ref[...].astype(F32)
    stores = []
    for side in range(2):
        turned = []
        for j in range(3 * side, 3 * side + 3):
            turned.append(jnp.transpose(rows_ref[pl.ds(j, lines, stride=MAIN), :].astype(BF16)))
        result = dot(jnp.concatenate(turned, axis=0), filt, (1, 1)).astype(BF16)
        for t in range(3):
            out_ref[3 * side + t] = result[LANES * t : LANES * t + WIDTH]
            out_ref[MAIN + side, PIECE * t : PIECE * (t + 1), :] = result[LANES * t + WIDTH : LANES * (t + 1)]
        for n, span in enumerate((pl.ds(3 * side, 3), pl.ds(MAIN + side, 1))):
            stores.append(pltpu.make_async_copy(out_ref.at[span], out_hbm.at[span], sems.at[2 * side + n]))
            stores[-1].start()
    for store in stores:
        store.wait()


def middle_kernel(
    rows_in_ref, filter_ref, norm_ref, weight_ref, out_ref, rows_ref, stage_ref, tiled_ref, *, tiles, owners
):
    blocks = tiled_ref.shape[0]
    for n in range(blocks):
        tiled_ref[n] = norm_ref[:, :, LANES * n : LANES * (n + 1)]
    block = owners * MESSAGE
    rows_ref[...] = rows_in_ref[...].astype(F32)

    def arrived(g, r, j):
        return rows_ref[pl.ds(block * g + MAIN * r + j, owners, stride=MESSAGE), :]

    def scales(r):
        parts = []
        for c in range(COMPS):
            pieces = [tiled_ref.at[n, r][pl.ds(c, owners, stride=COMPS), :] for n in range(blocks)]
            parts.append(jnp.concatenate(pieces, axis=1))
        return jnp.concatenate(parts, axis=0)

    lines = []
    for r in range(ROWS):
        rows = [[arrived(g, r, j) for j in range(MAIN)] for g in range(tiles)]
        for j in range(MAIN):
            lines.append(jnp.concatenate([row[j][:, :WIDTH] for row in rows], axis=1).astype(BF16))
        for i in range(2):
            pieces = [row[3 * i + t][:, WIDTH:] for row in rows for t in range(3)]
            lines.append(jnp.concatenate(pieces, axis=1).astype(BF16))
    filt = filter_ref[...]
    second = dot(jnp.concatenate(lines, axis=0), filt, (1, 0)).astype(BF16).astype(F32)
    comps = owners * COMPS
    raised = []
    for r in range(ROWS):
        scaled = scales(r) * second[r * comps : (r + 1) * comps]
        upper = scaled.astype(BF16)
        under = (scaled - upper.astype(F32)).astype(BF16)
        product = dot(weight_ref[...], jnp.concatenate([upper, under, upper], axis=0), (1, 0))
        raised.append((scales(r) * product).astype(BF16))
    middle = jnp.concatenate(raised, axis=0)
    lane = lax.broadcasted_iota(jnp.int32, (owners, LANES), 1)
    half = tiles // 2
    for g in range(tiles):
        if g % half == 0:
            third = dot(middle, filt[WIDTH * g : WIDTH * (g + half)], (1, 1))
        start = WIDTH * (g % half)
        for r in range(ROWS):
            for j in range(MAIN):
                line = r * comps + j * owners
                piece = third[line : line + owners, start : start + WIDTH]
                piece = jnp.concatenate([piece, jnp.zeros((owners, PIECE), F32)], axis=1)
                line = r * comps + (MAIN + j // 3) * owners
                at = start + PIECE * (j % 3)
                tile = third[line : line + owners, at - at % LANES : at - at % LANES + LANES]
                tile = pltpu.roll(tile, (WIDTH - at) % LANES, 1)
                stage_ref.at[g % 2][pl.ds(MAIN * r + j, owners, stride=MESSAGE), :] = jnp.where(lane < WIDTH, piece, tile)
        out_ref[block * g : block * (g + 1), :] = stage_ref[g % 2].astype(BF16)


VMEM = pl.BlockSpec(memory_space=pltpu.VMEM)
HBM = pl.BlockSpec(memory_space=pltpu.HBM)
SPREAD_FLOPS = 2 * 10**10


def per_device(tiles, owners, field, norm_field, vertical, x_filter, y_filter):
    lines, comps, width = field.shape
    total = tiles * owners * MESSAGE
    message_rows = jax.ShapeDtypeStruct((total, LANES), BF16)
    rows_scratch = pltpu.VMEM((total, LANES), F32)
    field_scratch = pltpu.VMEM((comps, width, lines), BF16)
    sems = pltpu.SemaphoreType.DMA

    def call(kernel, name, out_shape, in_specs, out_specs, scratch, *operands, flops):
        return pl.pallas_call(
            kernel,
            out_shape=out_shape,
            in_specs=in_specs,
            out_specs=out_specs,
            scratch_shapes=scratch,
            compiler_params=pltpu.CompilerParams(vmem_limit_bytes=40 * 1024 * 1024),
            cost_estimate=pl.CostEstimate(flops=flops, bytes_accessed=sum(a.nbytes for a in operands), transcendentals=0),
            name=name,
        )(*operands)

    def exchange(rows):
        grouped = rows.reshape(tiles * owners, MESSAGE // 2, 2, LANES)
        moved = lax.all_to_all(grouped, ("gx", "gy"), split_axis=0, concat_axis=0, tiled=True)
        return moved.reshape(total, LANES)

    def in_hbm(array):
        return pltpu.with_memory_space_constraint(array, pltpu.HBM)

    levels = vertical.shape[0] * vertical.shape[1]
    weight = jax.ShapeDtypeStruct((levels, 3 * levels), BF16)
    scratch = [field_scratch] + [pltpu.VMEM(a.shape, a.dtype) for a in (y_filter, vertical)] + [rows_scratch, sems((3,))]
    operands = [in_hbm(a) for a in (jnp.transpose(field, (1, 2, 0)), y_filter, vertical)]
    out = (message_rows, weight)
    rows, weight = call(spread_kernel, "spread", out, [HBM] * 3, (VMEM, VMEM), scratch, *operands, flops=SPREAD_FLOPS)
    rows = exchange(rows)
    blocks = x_filter.shape[0] // LANES
    norm_scratch = pltpu.VMEM((blocks, ROWS, levels, LANES), F32)
    scratch = [rows_scratch, pltpu.VMEM((2, owners * MESSAGE, LANES), F32), norm_scratch]
    middle = functools.partial(middle_kernel, tiles=tiles, owners=owners)
    operands = (rows, x_filter, norm_field, weight)
    rows = call(middle, "middle", message_rows, [VMEM] * 4, VMEM, scratch, *operands, flops=5 * 10**9)
    rows = exchange(rows)
    result = jax.ShapeDtypeStruct((comps, width, lines), BF16)
    result = call(gather_kernel, "gather", result, [VMEM, VMEM], HBM, [rows_scratch, field_scratch, sems((4,))], rows, y_filter, flops=10**9)
    return jnp.transpose(result, (2, 0, 1))


def solution(mesh):
    return jax.shard_map(
        functools.partial(per_device, mesh.shape["gx"], mesh.shape["gy"]),
        mesh=mesh,
        in_specs=(P(None, "gy", "gx"), P(("gx", "gy"), None, None), P(), P(), P()),
        out_specs=P(None, "gy", "gx"),
        check_vma=False,
    )
```
